32 devices in a mesh: runs: 2 (over x), patch: 16 (over z, y, core).
Axes of the slice: x: 2, y: 2, z: 4, core: 2. Of those that a mesh axis runs over, the one named last changes fastest.
Arguments:
- state: float32 [128, 5, 32768], P(('runs', 'patch')), parts along dimension 0, may hold values from -1 to 6, as said below
- levels: int32 [128], P(('runs', 'patch')), parts along dimension 0, may hold values from 0 to 1
- neighbors: int32 [6, 128], P(None, ('runs', 'patch')), parts along dimension 1, may hold values from -1 to 63, as said below
- new_counts: int32 [32], P(('runs', 'patch')), parts along dimension 0, may hold values from 2 to 6, as said below
Outputs:
- advanced: float32 [192, 5, 32768], P(('runs', 'patch')), parts along dimension 0
- gravity: float32 [3, 128], P(None, ('runs', 'patch')), parts along dimension 1
The draws below stay inside these ranges and needn't reach their ends.
There are 2 independent parts, one for each index of `runs`. The reference program is written for one: setup_inputs(seed, part) draws one part's arguments, and reference() takes and returns one part's arrays. A program takes and returns all parts, laid end to end along the dimension named above; each array names one. Nothing has to cross between parts.
Inputs may be any that keep to these rules, and one draw needn't show every extreme that they name: `state`: field 0 is density, fields 1 to 3 momentum, field 4 total energy; density and pressure 0.4 (E - |m|^2 / (2 rho)) lie in 0.5 to 2 and every velocity component in -0.5 to 0.5. `neighbors`: -1 marks a face on the domain's boundary; any other entry is a curve position less than the patch's own for low faces and greater for high faces, at most 2 away. `new_counts`: the entries sum to 64; for every device d the sum of the entries before d differs from d * 4 by at most 1; some device receives 3 * 2 positions.
All inputs are finite; a program needn't handle non-finite values.
Results may differ from the reference program's by a relative error of at most 0.0003.
Values sent between devices are 32-bit elements; how exact they have to be, the bound alone decides.
A program may use at most 128 MiB of HBM per device.

```python
import jax
import jax.numpy as jnp
from jax import lax

FIELDS = 5
EDGE = 32
SLOTS = 4
CELLS = 32768
NPATCH = 64
CAP = 6
N_PATCH = 16


def draw_state(key, part):
    key = jax.random.fold_in(key, 11)
    subkeys = jax.random.split(key, 3)
    grid_shape = (NPATCH, CELLS)
    density = jax.random.uniform(subkeys[0], grid_shape, dtype=jnp.float32, minval=0.5, maxval=2.0)
    pressure = jax.random.uniform(subkeys[1], grid_shape, dtype=jnp.float32, minval=0.5, maxval=2.0)
    velocity = jax.random.uniform(subkeys[2], (3, NPATCH, CELLS), dtype=jnp.float32, minval=-0.5, maxval=0.5)
    energy = pressure / 0.4 + 0.5 * density * (velocity[0] * velocity[0] + velocity[1] * velocity[1] + velocity[2] * velocity[2])
    stacked = jnp.stack([density, density * velocity[0], density * velocity[1], density * velocity[2], energy], axis=1)
    return stacked.astype(jnp.float32)


def draw_neighbors(key, part):
    key = jax.random.fold_in(key, 37)
    key_one, key_two = jax.random.split(key)
    offsets = jax.random.randint(key_one, (6, NPATCH), 1, SLOTS // 2 + 1)
    face_signs = jnp.where(jnp.arange(6, dtype=jnp.int32) % 2 == 0, -1, 1)
    positions = jnp.arange(NPATCH, dtype=jnp.int32)
    targets = positions[None, :] + face_signs[:, None] * offsets
    boundary = jax.random.randint(key_two, (6, NPATCH), 0, 8) == 0
    outside = (targets < 0) | (targets >= NPATCH) | boundary
    return jnp.where(outside, -1, targets).astype(jnp.int32)


def draw_new_counts(key, part):
    key = jax.random.fold_in(key, 23)
    key_one, key_two = jax.random.split(key)
    quarter = SLOTS // 4
    interior = jax.random.randint(key_one, (N_PATCH - 1,), -quarter, quarter + 1)
    chosen = jax.random.randint(key_two, (), 1, N_PATCH - 1)
    places = jnp.arange(N_PATCH - 1, dtype=jnp.int32)
    interior = jnp.where(places == chosen - 1, -quarter, interior)
    interior = jnp.where(places == chosen, quarter, interior)
    nothing = jnp.zeros((1,), jnp.int32)
    drifts = jnp.concatenate([nothing, interior.astype(jnp.int32), nothing])
    return (SLOTS + drifts[1:] - drifts[:-1]).astype(jnp.int32)


def with_ends(array, stream_key, smallest, high):
    index_at = [jax.random.randint(jax.random.fold_in(stream_key, axis), (), 0, length) for axis, length in enumerate(array.shape)]
    widest = array.shape.index(max(array.shape))
    next_to = index_at[:widest] + [(index_at[widest] + 1) % array.shape[widest]] + index_at[widest + 1:]
    return array.at[tuple(index_at)].set(smallest).at[tuple(next_to)].set(high)


def setup_inputs(seed: int = 0, part: int = 0) -> dict:
    splits = jax.random.split(jax.random.key(seed), 5)
    part_keys = jax.random.split(jax.random.fold_in(splits[4], part), 5)
    return {
        "state": draw_state(jax.random.fold_in(jax.random.fold_in(splits[4], part), 71), part),
        "levels": with_ends(jax.random.randint(part_keys[1], (NPATCH,), 0, 2), jax.random.fold_in(part_keys[1], 1), 0, 1).astype(jnp.int32),
        "neighbors": draw_neighbors(jax.random.fold_in(jax.random.fold_in(splits[4], part), 71), part),
        "new_counts": draw_new_counts(jax.random.fold_in(jax.random.fold_in(splits[4], part), 71), part),
    }


GAMMA = 1.4
DT_STEP = 0.01
GRAV_C = 2.0
SOFTEN = 0.25

def flux_speed(conserved, direction):
    density = conserved[:, 0]
    moment = conserved[:, direction + 1]
    velocity = moment / density
    kinetic = 0.5 * (conserved[:, 1] * conserved[:, 1] + conserved[:, 2] * conserved[:, 2] + conserved[:, 3] * conserved[:, 3]) / density
    pressure = (GAMMA - 1.0) * (conserved[:, 4] - kinetic)
    sound_speed = jnp.sqrt(GAMMA * pressure / density)
    pieces = [moment]
    for component in range(3):
        summand = conserved[:, component + 1] * velocity
        if component == direction:
            summand = summand + pressure
        pieces.append(summand)
    pieces.append((conserved[:, 4] + pressure) * velocity)
    return (jnp.stack(pieces, axis=1), jnp.abs(velocity) + sound_speed)

def rusanov(lower_state, upper_state, direction):
    flux_lower, speed_lower = flux_speed(lower_state, direction)
    flux_upper, speed_upper = flux_speed(upper_state, direction)
    wave_speed = jnp.maximum(speed_lower, speed_upper)
    return 0.5 * (flux_lower + flux_upper) - 0.5 * wave_speed[:, None] * (upper_state - lower_state)

def face_layers(fields_now):
    patch_count, field_count, edge_cells, plane_cells = fields_now.shape
    cube_view = fields_now.reshape(patch_count, field_count, edge_cells, edge_cells, edge_cells)
    layers = [fields_now[:, :, 0], fields_now[:, :, edge_cells - 1], cube_view[:, :, :, 0].reshape(patch_count, field_count, plane_cells), cube_view[:, :, :, edge_cells - 1].reshape(patch_count, field_count, plane_cells), cube_view[:, :, :, :, 0].reshape(patch_count, field_count, plane_cells), cube_view[:, :, :, :, edge_cells - 1].reshape(patch_count, field_count, plane_cells)]
    return jnp.stack(layers, axis=1)

def collect(buffer, face_data, neighbor_ids, slot_index):
    ghosts = []
    for face_number in range(6):
        chosen = buffer[slot_index[face_number], face_number ^ 1]
        present = neighbor_ids[face_number] >= 0
        ghosts.append(jnp.where(present[:, None, None], chosen, face_data[:, face_number]))
    return ghosts

def euler_update(fields_now, face_data, ghosts, step_ratio, accel):
    patch_count, field_count, edge_cells, plane_cells = fields_now.shape
    column = lax.broadcasted_iota(jnp.int32, (plane_cells,), 0)
    row_y = column // edge_cells
    row_z = column % edge_cells

    def spread_y(face_layer):
        return jnp.tile(face_layer.reshape(patch_count, field_count, edge_cells, edge_cells), (1, 1, 1, edge_cells))

    def spread_z(face_layer):
        return jnp.repeat(face_layer.reshape(patch_count, field_count, edge_cells, edge_cells), edge_cells, axis=3)
    below_x = jnp.concatenate([ghosts[0][:, :, None], fields_now[:, :, :-1]], axis=2)
    lower_x = rusanov(below_x, fields_now, 0)
    edge_x = rusanov(face_data[:, 1], ghosts[1], 0)
    upper_x = jnp.concatenate([lower_x[:, :, 1:], edge_x[:, :, None]], axis=2)
    below_y = jnp.where(row_y == 0, spread_y(ghosts[2]), jnp.roll(fields_now, edge_cells, axis=3))
    lower_y = rusanov(below_y, fields_now, 1)
    edge_y = rusanov(face_data[:, 3], ghosts[3], 1)
    upper_y = jnp.where(row_y == edge_cells - 1, spread_y(edge_y), jnp.roll(lower_y, -edge_cells, axis=3))
    below_z = jnp.where(row_z == 0, spread_z(ghosts[4]), jnp.roll(fields_now, 1, axis=3))
    lower_z = rusanov(below_z, fields_now, 2)
    edge_z = rusanov(face_data[:, 5], ghosts[5], 2)
    upper_z = jnp.where(row_z == edge_cells - 1, spread_z(edge_z), jnp.roll(lower_z, -1, axis=3))
    divergence = upper_x - lower_x + (upper_y - lower_y) + (upper_z - lower_z)
    density = fields_now[:, 0]
    pull_x = accel[0][:, None, None]
    pull_y = accel[1][:, None, None]
    pull_z = accel[2][:, None, None]
    source = jnp.stack([jnp.zeros_like(density), density * pull_x, density * pull_y, density * pull_z, fields_now[:, 1] * pull_x + fields_now[:, 2] * pull_y + fields_now[:, 3] * pull_z], axis=1)
    return fields_now - step_ratio[:, None, None, None] * divergence + DT_STEP * source

def curve_coords(positions, total_bits):
    coords = [jnp.zeros_like(positions), jnp.zeros_like(positions), jnp.zeros_like(positions)]
    for bit_index in range(total_bits):
        bit_value = positions // 2 ** bit_index % 2
        coords[bit_index % 3] = coords[bit_index % 3] + bit_value * 2 ** (bit_index // 3)
    return [coords[0].astype(jnp.float32) + 0.5, coords[1].astype(jnp.float32) + 0.5, coords[2].astype(jnp.float32) + 0.5]

def gravity_at(positions, masses, npatch):
    total_bits = npatch.bit_length() - 1
    target = curve_coords(positions, total_bits)
    sources = curve_coords(jnp.arange(npatch, dtype=jnp.int32), total_bits)
    offsets = [sources[axis_number][None, :] - target[axis_number][:, None] for axis_number in range(3)]
    distance = offsets[0] * offsets[0] + offsets[1] * offsets[1] + offsets[2] * offsets[2] + SOFTEN
    weight = masses[None, :] / (distance * jnp.sqrt(distance))
    strength = GRAV_C / float(npatch) ** (1.0 / 3.0)
    return jnp.stack([strength * lax.optimization_barrier(jnp.sum(weight * offsets[axis_number], axis=1)) for axis_number in range(3)], axis=0)

def patch_mass(state, levels):
    return lax.optimization_barrier(jnp.mean(state[:, 0, :], axis=1)) * jnp.exp2(-3.0 * levels.astype(jnp.float32))

def ratio_of(levels):
    return 0.025 * jnp.exp2(levels.astype(jnp.float32))

def reference(state, levels, neighbors, new_counts):
    npatch = state.shape[0]
    block_size = min(16, npatch)
    block_total = npatch // block_size
    masses = patch_mass(state, levels)

    def gravity_block(block_index):
        positions = block_index * block_size + jnp.arange(block_size, dtype=jnp.int32)
        return gravity_at(positions, masses, npatch)
    gravity = lax.map(gravity_block, jnp.arange(block_total, dtype=jnp.int32))
    gravity = jnp.transpose(gravity, (1, 0, 2)).reshape(3, npatch)
    step_ratio = ratio_of(levels)

    def run_section(fields_all):
        shaped = fields_all.reshape(npatch, FIELDS, EDGE, EDGE * EDGE)
        faces_all = face_layers(shaped)

        def one_block(block_index):
            block_start = block_index * block_size
            block_cells = lax.dynamic_slice_in_dim(shaped, block_start, block_size, 0)
            own_faces = lax.dynamic_slice_in_dim(faces_all, block_start, block_size, 0)
            neighbor_ids = lax.dynamic_slice_in_dim(neighbors, block_start, block_size, 1)
            ghosts = collect(faces_all, own_faces, neighbor_ids, jnp.clip(neighbor_ids, 0, npatch - 1))
            block_ratio = lax.dynamic_slice_in_dim(step_ratio, block_start, block_size, 0)
            block_pull = lax.dynamic_slice_in_dim(gravity, block_start, block_size, 1)
            return euler_update(block_cells, own_faces, ghosts, block_ratio, block_pull)
        updated = lax.map(one_block, jnp.arange(block_total, dtype=jnp.int32))
        return updated.reshape(fields_all.shape)
    section_one = run_section(state)
    final = 0.5 * state + 0.5 * run_section(section_one)
    starts = jnp.cumsum(new_counts) - new_counts
    slot_ids = jnp.arange(CAP, dtype=jnp.int32)
    source_index = (starts[:, None] + slot_ids[None, :]).astype(jnp.int32)
    occupied = (slot_ids[None, :] < new_counts[:, None]).reshape(-1)
    gathered = final[jnp.clip(source_index, 0, npatch - 1).reshape(-1)]
    advanced = jnp.where(occupied[:, None, None], gathered, jnp.zeros_like(gathered))
    return (advanced, gravity)
```

```python
import jax
import jax.numpy as jnp
from jax import lax
from jax.experimental import pallas as pl
from jax.experimental.pallas import tpu as pltpu
from jax.sharding import PartitionSpec as P

FIELDS = 5
EDGE = 32
CAP = 6
LANES = 128
ROWS = 8
PLANES = 32
TILES = 256

GAMMA = 1.4
DT_STEP = 0.01
GRAV_C = 2.0
SOFTEN = 0.25
UNROLL = 4


def primitives(u):
    density, m1, m2, m3, energy = u
    inverse = pl.reciprocal(density, approx=True)
    inverse = inverse * (2.0 - density * inverse)
    velocity = [m1 * inverse, m2 * inverse, m3 * inverse]
    twice_kinetic = m1 * velocity[0] + m2 * velocity[1] + m3 * velocity[2]
    pressure = (GAMMA - 1.0) * energy - (0.5 * (GAMMA - 1.0)) * twice_kinetic
    square = GAMMA * pressure * inverse
    sound = square * lax.rsqrt(jnp.maximum(square, 1e-30))
    return velocity, pressure, sound, energy + pressure


def flux(u, prim, k):
    velocity, pressure, sound, enthalpy = prim
    speed = velocity[k]
    out = [u[k + 1]]
    for c in range(3):
        term = u[c + 1] * speed
        out.append(term + pressure if c == k else term)
    out.append(enthalpy * speed)
    return out, jnp.abs(speed) + sound


def interface(lower, upper):
    u_l, f_l, s_l = lower
    u_r, f_r, s_r = upper
    wave = jnp.maximum(s_l, s_r)
    return [(f_l[i] + f_r[i]) - wave * (u_r[i] - u_l[i]) for i in range(FIELDS)]


def with_flux(u, k):
    f, s = flux(u, primitives(u), k)
    return u, f, s


def iotas():
    sub = lax.broadcasted_iota(jnp.int32, (ROWS, LANES), 0)
    lane = lax.broadcasted_iota(jnp.int32, (ROWS, LANES), 1)
    return sub, lane


def curve_coords(positions, bits):
    coords = [jnp.zeros_like(positions) for _ in range(3)]
    for b in range(bits):
        coords[b % 3] = coords[b % 3] + ((positions >> b) & 1) * 2 ** (b // 3)
    return [c.astype(jnp.float32) for c in coords]


def make_kernel(devices, held):
    npatch = devices * held
    bits = npatch.bit_length() - 1
    strength = GRAV_C / float(npatch) ** (1.0 / 3.0)
    window = held // 2
    low_own, low_far = 0, held
    high_far, high_own = held + window, held + 2 * window

    def kernel(
        state, levels, neighbors, counts,
        ext, grav_out, info_out,
        tin, u0, s1, fin, faces1, faces2, msg, gath, edge_z, edge_y,
        in_sem, out_sem, mass_send, mass_recv, f_send, f_recv, g_send, g_recv,
    ):
        me = lax.axis_index("patch")
        run = lax.axis_index("runs")
        sub, lane = iotas()
        lane_z = lane & (EDGE - 1)
        has_low = me > 0
        has_high = me < devices - 1

        barrier = pltpu.get_barrier_semaphore()

        def greet(i, _):
            pl.semaphore_signal(
                barrier, inc=1, device_id=(run, lax.rem(me + i, devices)),
                device_id_type=pl.DeviceIdType.MESH,
            )
            return 0

        lax.fori_loop(1, devices, greet, 0)
        loads = [
            pltpu.make_async_copy(state.at[f], tin.at[f], in_sem.at[f]) for f in range(FIELDS)
        ]
        for c in loads:
            c.start()
        for c in loads:
            c.wait()

        def plane(ref, p, f, x):
            return ref[p, f, pl.ds(pl.multiple_of(x * ROWS, ROWS), ROWS), :]

        def pack_faces(p, ref, faces):
            for f in range(FIELDS):
                faces[low_own + p, 0, f] = ref[p, f, pl.ds(0, ROWS), :]
                faces[high_own + p, 0, f] = ref[p, f, pl.ds((PLANES - 1) * ROWS, ROWS), :]
                low_y = ref[p, f, pl.ds(0, ROWS, stride=ROWS), :]
                high_y = pltpu.roll(ref[p, f, pl.ds(ROWS - 1, ROWS, stride=ROWS), :], 32, 1)
                for g in range(1, 4):
                    at = g * ROWS * ROWS
                    inside = (lane >> 5) == g
                    more = ref[p, f, pl.ds(at, ROWS, stride=ROWS), :]
                    low_y = jnp.where(inside, pltpu.roll(more, 32 * g, 1), low_y)
                    more = ref[p, f, pl.ds(at + ROWS - 1, ROWS, stride=ROWS), :]
                    high_y = jnp.where(inside, pltpu.roll(more, 32 * (g + 1) % LANES, 1), high_y)
                faces[low_own + p, 1, f] = low_y
                faces[high_own + p, 1, f] = high_y
                low_z = ref[p, f, pl.ds(0, ROWS), :]
                high_z = pltpu.roll(low_z, LANES - 31, 1)
                for x in range(1, PLANES):
                    here = lane_z == x
                    now = ref[p, f, pl.ds(x * ROWS, ROWS), :]
                    low_z = jnp.where(here, pltpu.roll(now, x, 1), low_z)
                    turned = now if x == 31 else pltpu.roll(now, LANES + x - 31, 1)
                    high_z = jnp.where(here, turned, high_z)
                faces[low_own + p, 2, f] = low_z
                faces[high_own + p, 2, f] = high_z

        def unpack(xb, totals):
            totals = list(totals)
            for i in range(2):
                at = pl.ds(pl.multiple_of((xb * 2 + i) * ROWS, ROWS), ROWS)
                for f in range(FIELDS):
                    for p in range(held):
                        v = tin[f, at, p, :]
                        u0[p, f, at, :] = v
                        if f == 0:
                            totals[p] = totals[p] + v
            return tuple(totals)

        zero = jnp.zeros((ROWS, LANES), jnp.float32)
        totals = lax.fori_loop(0, PLANES // 2, unpack, (zero,) * held)

        def pack_first(p, _):
            pack_faces(p, u0, faces1)
            return 0

        lax.fori_loop(0, held, pack_first, 0)
        message = jnp.where(sub == held, counts[0].astype(jnp.float32), 0.0)
        for p in range(held):
            total = jnp.sum(jnp.sum(totals[p], axis=0, keepdims=True), axis=1, keepdims=True)
            level = jnp.full((ROWS, LANES), levels[p].astype(jnp.float32))
            mass = jnp.broadcast_to(total, (ROWS, LANES)) * (1.0 / (LANES * TILES))
            message = jnp.where(sub == p, mass * jnp.exp2(-3.0 * level), message)
        msg[...] = message
        gath[me] = message
        pl.semaphore_wait(barrier, devices - 1)

        def mass_copy(target, slot, s_sem, r_sem):
            return pltpu.make_async_remote_copy(
                src_ref=msg, dst_ref=gath.at[slot], send_sem=s_sem, recv_sem=r_sem,
                device_id=(run, target), device_id_type=pl.DeviceIdType.MESH,
            )

        def face_copies(faces, send, recv):
            down = pltpu.make_async_remote_copy(
                src_ref=faces.at[pl.ds(low_own, window)],
                dst_ref=faces.at[pl.ds(low_far, window)],
                send_sem=send.at[0], recv_sem=recv.at[0],
                device_id=(run, me - 1), device_id_type=pl.DeviceIdType.MESH,
            )
            up = pltpu.make_async_remote_copy(
                src_ref=faces.at[pl.ds(high_own + held - window, window)],
                dst_ref=faces.at[pl.ds(high_far, window)],
                send_sem=send.at[1], recv_sem=recv.at[1],
                device_id=(run, me + 1), device_id_type=pl.DeviceIdType.MESH,
            )
            return down, up

        def start_both(pair):
            pl.when(has_low)(lambda: pair[0].start())
            pl.when(has_high)(lambda: pair[1].start())

        def wait_both(pair):
            pl.when(has_low)(lambda: pair[0].wait_send())
            pl.when(has_high)(lambda: pair[1].wait_send())
            pl.when(has_high)(lambda: pair[0].wait_recv())
            pl.when(has_low)(lambda: pair[1].wait_recv())

        pair1 = face_copies(faces1, f_send.at[0], f_recv.at[0])
        start_both(pair1)

        def send_mass(i, _):
            target = lax.rem(me + i, devices)
            mass_copy(target, me, mass_send.at[i], mass_recv.at[me]).start()
            return 0

        lax.fori_loop(1, devices, send_mass, 0)

        def wait_mass(i, _):
            source = lax.rem(me + i, devices)
            c = mass_copy(source, source, mass_send.at[i], mass_recv.at[source])
            c.wait_send()
            c.wait_recv()
            return 0

        lax.fori_loop(1, devices, wait_mass, 0)

        target = curve_coords(me * held + (lane & (held - 1)), bits)

        def pull(j, sums):
            got_mass = gath[j]
            source = curve_coords(j * held + (sub & (held - 1)), bits)
            off = [source[a] - target[a] for a in range(3)]
            d = off[0] * off[0] + off[1] * off[1] + off[2] * off[2] + SOFTEN
            inv = lax.rsqrt(d)
            w = jnp.where(sub < held, got_mass, 0.0) * (inv * inv * inv)
            is_count = sub == held
            start = sums[3] + jnp.where(is_count & (j < me), got_mass, 0.0)
            count = sums[4] + jnp.where(is_count & (j == me), got_mass, 0.0)
            return tuple(sums[a] + w * off[a] for a in range(3)) + (start, count)

        sums = lax.fori_loop(0, devices, pull, (zero,) * 5)
        sums = [jnp.broadcast_to(jnp.sum(s, axis=0, keepdims=True), (ROWS, LANES)) for s in sums]
        accel = [strength * s for s in sums[:3]]
        grav_out[...] = jnp.where(sub == 0, accel[0], jnp.where(sub == 1, accel[1], accel[2]))
        offset = sums[3].astype(jnp.int32) - me * held + 1
        info_out[...] = jnp.where(lane == 0, offset, sums[4].astype(jnp.int32))

        def advance(p, ref, faces, write):
            level = jnp.full((ROWS, LANES), levels[p].astype(jnp.float32))
            half_ratio = 0.0125 * jnp.exp2(level)
            g = [
                DT_STEP * jnp.broadcast_to(
                    jnp.sum(jnp.where(lane == p, accel[a], 0.0), axis=1, keepdims=True),
                    (ROWS, LANES),
                )
                for a in range(3)
            ]

            def ghost(f, axis):
                nb = neighbors[f, p]
                if f % 2 == 0:
                    slot = jnp.where(nb >= 0, nb - me * held + high_own, low_own + p)
                else:
                    slot = jnp.where(nb >= 0, nb - me * held, high_own + p)
                slot = jnp.clip(slot, 0, 2 * held + 2 * window - 1)
                return [faces[slot, axis, i] for i in range(FIELDS)]

            def own(high, axis):
                base = (high_own if high else low_own) + p
                return [faces[base, axis, i] for i in range(FIELDS)]

            z_low = interface(with_flux(ghost(4, 2), 2), with_flux(own(False, 2), 2))
            z_high = interface(with_flux(own(True, 2), 2), with_flux(ghost(5, 2), 2))
            y_low = interface(with_flux(ghost(2, 1), 1), with_flux(own(False, 1), 1))
            y_high = interface(with_flux(own(True, 1), 1), with_flux(ghost(3, 1), 1))
            for f in range(FIELDS):
                edge_z[0, f] = z_low[f]
                edge_z[1, f] = z_high[f]
                for q in range(4):
                    low = y_low[f] if q == 0 else pltpu.roll(y_low[f], LANES - 32 * q, 1)
                    high = y_high[f] if q == 3 else pltpu.roll(y_high[f], 96 - 32 * q, 1)
                    edge_y[0, f, pl.ds(q * ROWS, ROWS), :] = low
                    edge_y[1, f, pl.ds(q * ROWS, ROWS), :] = high
            before = with_flux(ghost(0, 0), 0)
            pending = [zero] * FIELDS

            at_z0 = lane_z == 0
            at_z31 = lane_z == EDGE - 1
            at_y0 = (sub == 0) & (lane < 32)
            at_y31 = (sub == ROWS - 1) & (lane >= 96)
            carry_low = lane < 32
            carry_high = lane >= 96

            def back_z(v):
                return pltpu.roll(v, 1, 1)

            def ahead_z(v):
                return pltpu.roll(v, LANES - 1, 1)

            def back_y(v):
                t = pltpu.roll(v, 32, 1)
                return jnp.where(carry_low, pltpu.roll(t, 1, 0), t)

            def ahead_y(v):
                t = pltpu.roll(v, LANES - 32, 1)
                return jnp.where(carry_high, pltpu.roll(t, ROWS - 1, 0), t)

            def shifted(u, f, s, k, move):
                mu = [move(v) for v in u]
                mf = [mu[k + 1]] + [move(v) for v in f[1:]]
                return mu, mf, move(s)

            def one(x, before, pending):
                u = [plane(ref, p, f, x) for f in range(FIELDS)]
                prim = primitives(u)
                fx, sx = flux(u, prim, 0)
                gx = interface(before, (u, fx, sx))
                write(p, jnp.maximum(x - 1, 0),
                      [pending[f] - half_ratio * gx[f] for f in range(FIELDS)])
                fy, sy = flux(u, prim, 1)
                gy = interface(shifted(u, fy, sy, 1, back_y), (u, fy, sy))
                fz, sz = flux(u, prim, 2)
                gz = interface(shifted(u, fz, sz, 2, back_z), (u, fz, sz))
                fresh = []
                for f in range(FIELDS):
                    ey0 = edge_y[0, f, pl.ds(x, 1), :]
                    ey1 = edge_y[1, f, pl.ds(x, 1), :]
                    ez0 = pltpu.roll(edge_z[0, f], LANES - x, 1)
                    ez1 = pltpu.roll(edge_z[1, f], LANES + 31 - x, 1)
                    div = jnp.where(at_y31, ey1, ahead_y(gy[f])) - jnp.where(at_y0, ey0, gy[f])
                    div += jnp.where(at_z31, ez1, ahead_z(gz[f])) - jnp.where(at_z0, ez0, gz[f])
                    fresh.append(u[f] - half_ratio * (div - gx[f]))
                for a in range(3):
                    fresh[a + 1] += u[0] * g[a]
                fresh[4] += u[1] * g[0] + u[2] * g[1] + u[3] * g[2]
                return (u, fx, sx), fresh

            def block(xb, carry):
                bu, bf, bs, pend = carry
                before, pend = (list(bu), list(bf), bs), list(pend)
                for i in range(UNROLL):
                    before, pend = one(xb * UNROLL + i, before, pend)
                return tuple(before[0]), tuple(before[1]), before[2], tuple(pend)

            carry = (tuple(before[0]), tuple(before[1]), before[2], tuple(pending))
            bu, bf, bs, pend = lax.fori_loop(0, PLANES // UNROLL, block, carry)
            gx = interface((bu, bf, bs), with_flux(ghost(1, 0), 0))
            write(p, PLANES - 1, [pend[f] - half_ratio * gx[f] for f in range(FIELDS)])

        def rows_of(x):
            return pl.ds(pl.multiple_of(x * ROWS, ROWS), ROWS)

        def write_one(p, x, values):
            for f in range(FIELDS):
                s1[p, f, rows_of(x), :] = values[f]

        def write_two(p, x, values):
            for f in range(FIELDS):
                fin[p, f, rows_of(x), :] = 0.5 * (plane(u0, p, f, x) + values[f])

        wait_both(pair1)

        def stage_one(p, _):
            advance(p, u0, faces1, write_one)
            pack_faces(p, s1, faces2)
            return 0

        lax.fori_loop(0, held, stage_one, 0)
        pair2 = face_copies(faces2, f_send.at[1], f_recv.at[1])
        start_both(pair2)
        wait_both(pair2)

        def patch_copies():
            down = pltpu.make_async_remote_copy(
                src_ref=fin.at[0], dst_ref=ext.at[held + 1],
                send_sem=g_send.at[0], recv_sem=g_recv.at[0],
                device_id=(run, me - 1), device_id_type=pl.DeviceIdType.MESH,
            )
            up = pltpu.make_async_remote_copy(
                src_ref=fin.at[held - 1], dst_ref=ext.at[0],
                send_sem=g_send.at[1], recv_sem=g_recv.at[1],
                device_id=(run, me + 1), device_id_type=pl.DeviceIdType.MESH,
            )
            return down, up

        pair3 = patch_copies()

        def keep(p):
            return pltpu.make_async_copy(fin.at[p], ext.at[p + 1], out_sem.at[p])

        def stage_two(i, _):
            p = lax.rem(i * (held - 1), held)
            advance(p, s1, faces2, write_two)
            keep(p).start()

            @pl.when(i == 1)
            def _():
                start_both(pair3)

            return 0

        lax.fori_loop(0, held, stage_two, 0)
        wait_both(pair3)
        for p in range(held):
            keep(p).wait()

    return kernel


def place_kernel(info, source, out):
    last = source.shape[0] - 1
    offset, count = info[0, 0], info[0, 1]
    for slot in range(CAP):
        used = slot < count
        at = jnp.minimum(slot + offset, last)

        def step(xb, _):
            for i in range(8):
                rows = pl.ds(pl.multiple_of((xb * 8 + i) * ROWS, ROWS), ROWS)
                out[0, rows, slot, :] = jnp.where(used, source[at, 0, rows, :], 0.0)
            return 0

        lax.fori_loop(0, PLANES // 8, step, 0)


def local(state, levels, neighbors, new_counts):
    held = state.shape[0]
    devices = lax.axis_size("patch")
    tiles = state.transpose(1, 0, 2).reshape(FIELDS, held, TILES, LANES).transpose(0, 2, 1, 3)
    f32 = jnp.float32
    smem = pl.BlockSpec(memory_space=pltpu.SMEM)
    vmem = pl.BlockSpec(memory_space=pltpu.VMEM)
    anyspace = pl.BlockSpec(memory_space=pl.ANY)
    dense = (held, FIELDS, TILES, LANES)
    faces = (2 * held + 2 * (held // 2), 3, FIELDS, ROWS, LANES)
    dma = pltpu.SemaphoreType.DMA
    ext, grav, info = pl.pallas_call(
        make_kernel(devices, held),
        out_shape=(
            jax.ShapeDtypeStruct((held + 2, FIELDS, TILES, LANES), f32),
            jax.ShapeDtypeStruct((ROWS, LANES), f32),
            jax.ShapeDtypeStruct((ROWS, LANES), jnp.int32),
        ),
        in_specs=[anyspace, smem, smem, smem],
        out_specs=(anyspace, vmem, vmem),
        scratch_shapes=[
            pltpu.VMEM((FIELDS, TILES, held, LANES), f32),
            pltpu.VMEM(dense, f32),
            pltpu.VMEM(dense, f32),
            pltpu.VMEM(dense, f32),
            pltpu.VMEM(faces, f32),
            pltpu.VMEM(faces, f32),
            pltpu.VMEM((ROWS, LANES), f32),
            pltpu.VMEM((devices, ROWS, LANES), f32),
            pltpu.VMEM((2, FIELDS, ROWS, LANES), f32),
            pltpu.VMEM((2, FIELDS, EDGE, LANES), f32),
            dma((FIELDS,)), dma((held,)),
            dma((devices,)), dma((devices,)),
            dma((2, 2)), dma((2, 2)),
            dma((2,)), dma((2,)),
        ],
        compiler_params=pltpu.CompilerParams(
            collective_id=0, has_side_effects=True, vmem_limit_bytes=48 * 2**20
        ),
        name="advance",
    )(tiles, levels, neighbors, new_counts)
    out = pl.pallas_call(
        place_kernel,
        out_shape=jax.ShapeDtypeStruct((FIELDS, TILES, CAP, LANES), f32),
        grid_spec=pltpu.PrefetchScalarGridSpec(
            num_scalar_prefetch=1,
            grid=(FIELDS,),
            in_specs=[
                pl.BlockSpec(
                    (held + 2, 1, TILES, LANES),
                    lambda f, info: (0, f, 0, 0),
                )
            ],
            out_specs=pl.BlockSpec((1, TILES, CAP, LANES), lambda f, info: (f, 0, 0, 0)),
        ),
        compiler_params=pltpu.CompilerParams(vmem_limit_bytes=60 * 2**20),
        name="place",
    )(info, ext)
    advanced = out.transpose(0, 2, 1, 3).reshape(FIELDS, CAP, TILES * LANES).transpose(1, 0, 2)
    return advanced, grav[:3, :held]


def solution(mesh):
    return jax.shard_map(
        local,
        mesh=mesh,
        in_specs=(
            P(("runs", "patch"), None, None),
            P(("runs", "patch")),
            P(None, ("runs", "patch")),
            P(("runs", "patch")),
        ),
        out_specs=(P(("runs", "patch"), None, None), P(None, ("runs", "patch"))),
        check_vma=False,
    )
```

```python
import jax
import jax.numpy as jnp
from jax import lax
from jax.experimental import pallas as pl
from jax.experimental.pallas import tpu as pltpu
from jax.sharding import PartitionSpec as P

FIELDS = 5
EDGE = 32
CAP = 6
LANES = 128
ROWS = 8
PLANES = 32
TILES = 256
PAD = 8

GAMMA = 1.4
DT_STEP = 0.01
GRAV_C = 2.0
SOFTEN = 0.25
UNROLL = 4


def primitives(u):
    density, m1, m2, m3, energy = u
    inverse = pl.reciprocal(density, approx=True)
    inverse = inverse * (2.0 - density * inverse)
    velocity = [m1 * inverse, m2 * inverse, m3 * inverse]
    twice_kinetic = m1 * velocity[0] + m2 * velocity[1] + m3 * velocity[2]
    pressure = (GAMMA - 1.0) * energy - (0.5 * (GAMMA - 1.0)) * twice_kinetic
    square = GAMMA * pressure * inverse
    sound = square * lax.rsqrt(jnp.maximum(square, 1e-30))
    return velocity, pressure, sound, energy + pressure


def flux(u, prim, k):
    velocity, pressure, sound, enthalpy = prim
    speed = velocity[k]
    out = [u[k + 1]]
    for c in range(3):
        term = u[c + 1] * speed
        out.append(term + pressure if c == k else term)
    out.append(enthalpy * speed)
    return out, jnp.abs(speed) + sound


def interface(lower, upper):
    u_l, f_l, s_l = lower
    u_r, f_r, s_r = upper
    wave = jnp.maximum(s_l, s_r)
    return [(f_l[i] + f_r[i]) - wave * (u_r[i] - u_l[i]) for i in range(FIELDS)]


def with_flux(u, k):
    f, s = flux(u, primitives(u), k)
    return u, f, s


def iotas():
    sub = lax.broadcasted_iota(jnp.int32, (ROWS, LANES), 0)
    lane = lax.broadcasted_iota(jnp.int32, (ROWS, LANES), 1)
    return sub, lane


def curve_coords(positions, bits):
    coords = [jnp.zeros_like(positions) for _ in range(3)]
    for b in range(bits):
        coords[b % 3] = coords[b % 3] + ((positions >> b) & 1) * 2 ** (b // 3)
    return [c.astype(jnp.float32) for c in coords]


def make_kernel(devices, held):
    npatch = devices * held
    bits = npatch.bit_length() - 1
    strength = GRAV_C / float(npatch) ** (1.0 / 3.0)
    window = held // 2

    def kernel(
        state, levels, neighbors, counts,
        ext, grav_out, info_out,
        tin, u0, s1, fin, own1, low1, high1, own2, low2, high2, msg, gath, edge_z, edge_y,
        in_sem, out_sem, mass_send, mass_recv, f_send, f_recv, g_send, g_recv,
    ):
        me = lax.axis_index("patch")
        run = lax.axis_index("runs")
        sub, lane = iotas()
        lane_z = lane & (EDGE - 1)
        has_low = me > 0
        has_high = me < devices - 1

        barrier = pltpu.get_barrier_semaphore()

        def greet(i, _):
            pl.semaphore_signal(
                barrier, inc=1, device_id=(run, lax.rem(me + i, devices)),
                device_id_type=pl.DeviceIdType.MESH,
            )
            return 0

        lax.fori_loop(1, devices, greet, 0)
        loads = [
            pltpu.make_async_copy(state.at[f], tin.at[f], in_sem.at[f]) for f in range(FIELDS)
        ]
        for c in loads:
            c.start()
        for c in loads:
            c.wait()

        def plane(ref, p, f, x):
            return ref[p, f, pl.ds(pl.multiple_of(x * ROWS + PAD, ROWS), ROWS), :]

        def plane_back(ref, p, f, x):
            return ref[p, f, pl.ds(pl.multiple_of(x * ROWS, ROWS) + (PAD - 1), ROWS), :]

        def pack_faces(p, ref, faces):
            for f in range(FIELDS):
                faces[p, 0, f] = ref[p, f, pl.ds(PAD, ROWS), :]
                faces[held + p, 0, f] = ref[p, f, pl.ds(PAD + (PLANES - 1) * ROWS, ROWS), :]
                low_y = ref[p, f, pl.ds(PAD, ROWS, stride=ROWS), :]
                high_y = pltpu.roll(ref[p, f, pl.ds(PAD + ROWS - 1, ROWS, stride=ROWS), :], 32, 1)
                for g in range(1, 4):
                    at = PAD + g * ROWS * ROWS
                    inside = (lane >> 5) == g
                    more = ref[p, f, pl.ds(at, ROWS, stride=ROWS), :]
                    low_y = jnp.where(inside, pltpu.roll(more, 32 * g, 1), low_y)
                    more = ref[p, f, pl.ds(at + ROWS - 1, ROWS, stride=ROWS), :]
                    high_y = jnp.where(inside, pltpu.roll(more, 32 * (g + 1) % LANES, 1), high_y)
                faces[p, 1, f] = low_y
                faces[held + p, 1, f] = high_y
                low_z = ref[p, f, pl.ds(PAD, ROWS), :]
                high_z = pltpu.roll(low_z, LANES - 31, 1)
                for x in range(1, PLANES):
                    here = lane_z == x
                    now = ref[p, f, pl.ds(PAD + x * ROWS, ROWS), :]
                    low_z = jnp.where(here, pltpu.roll(now, x, 1), low_z)
                    turned = now if x == 31 else pltpu.roll(now, LANES + x - 31, 1)
                    high_z = jnp.where(here, turned, high_z)
                faces[p, 2, f] = low_z
                faces[held + p, 2, f] = high_z

        def unpack(xb, totals):
            totals = list(totals)
            for i in range(2):
                x = xb * 2 + i
                at = pl.ds(pl.multiple_of(x * ROWS + PAD, ROWS), ROWS)
                for f in range(FIELDS):
                    for p in range(held):
                        v = tin[f, pl.ds(x * (held * ROWS) + p, ROWS, stride=held), :]
                        u0[p, f, at, :] = v
                        if f == 0:
                            totals[p] = totals[p] + v
            return tuple(totals)

        zero = jnp.zeros((ROWS, LANES), jnp.float32)
        totals = lax.fori_loop(0, PLANES // 2, unpack, (zero,) * held)

        def pack_first(p, _):
            pack_faces(p, u0, own1)
            return 0

        lax.fori_loop(0, held, pack_first, 0)
        message = jnp.where(sub == held, counts[0].astype(jnp.float32), 0.0)
        for p in range(held):
            total = jnp.sum(jnp.sum(totals[p], axis=0, keepdims=True), axis=1, keepdims=True)
            level = jnp.full((ROWS, LANES), levels[p].astype(jnp.float32))
            mass = jnp.broadcast_to(total, (ROWS, LANES)) * (1.0 / (LANES * TILES))
            message = jnp.where(sub == p, mass * jnp.exp2(-3.0 * level), message)
        msg[...] = message
        gath[me] = message
        pl.semaphore_wait(barrier, devices - 1)

        def mass_copy(target, slot, s_sem, r_sem):
            return pltpu.make_async_remote_copy(
                src_ref=msg, dst_ref=gath.at[slot], send_sem=s_sem, recv_sem=r_sem,
                device_id=(run, target), device_id_type=pl.DeviceIdType.MESH,
            )

        def face_copies(own, low, high, send, recv):
            down = pltpu.make_async_remote_copy(
                src_ref=own.at[pl.ds(0, window)], dst_ref=high,
                send_sem=send.at[0], recv_sem=recv.at[0],
                device_id=(run, me - 1), device_id_type=pl.DeviceIdType.MESH,
            )
            up = pltpu.make_async_remote_copy(
                src_ref=own.at[pl.ds(2 * held - window, window)], dst_ref=low,
                send_sem=send.at[1], recv_sem=recv.at[1],
                device_id=(run, me + 1), device_id_type=pl.DeviceIdType.MESH,
            )
            return down, up

        def start_down(pair):
            pl.when(has_low)(lambda: pair[0].start())

        def start_up(pair):
            pl.when(has_high)(lambda: pair[1].start())

        def wait_sent(pair):
            pl.when(has_low)(lambda: pair[0].wait_send())
            pl.when(has_high)(lambda: pair[1].wait_send())

        def wait_from_high(pair):
            pl.when(has_high)(lambda: pair[0].wait_recv())

        def wait_from_low(pair):
            pl.when(has_low)(lambda: pair[1].wait_recv())

        pair1 = face_copies(own1, low1, high1, f_send.at[0], f_recv.at[0])
        start_down(pair1)
        start_up(pair1)

        def send_mass(i, _):
            target = lax.rem(me + i, devices)
            mass_copy(target, me, mass_send.at[i], mass_recv.at[me]).start()
            return 0

        lax.fori_loop(1, devices, send_mass, 0)

        def wait_mass(i, _):
            source = lax.rem(me + i, devices)
            c = mass_copy(source, source, mass_send.at[i], mass_recv.at[source])
            c.wait_send()
            c.wait_recv()
            return 0

        lax.fori_loop(1, devices, wait_mass, 0)

        target = curve_coords(me * held + (lane & (held - 1)), bits)

        def pull(j, sums):
            got_mass = gath[j]
            source = curve_coords(j * held + (sub & (held - 1)), bits)
            off = [source[a] - target[a] for a in range(3)]
            d = off[0] * off[0] + off[1] * off[1] + off[2] * off[2] + SOFTEN
            inv = lax.rsqrt(d)
            w = jnp.where(sub < held, got_mass, 0.0) * (inv * inv * inv)
            is_count = sub == held
            start = sums[3] + jnp.where(is_count & (j < me), got_mass, 0.0)
            count = sums[4] + jnp.where(is_count & (j == me), got_mass, 0.0)
            return tuple(sums[a] + w * off[a] for a in range(3)) + (start, count)

        sums = lax.fori_loop(0, devices, pull, (zero,) * 5)
        sums = [jnp.broadcast_to(jnp.sum(s, axis=0, keepdims=True), (ROWS, LANES)) for s in sums]
        accel = [strength * s for s in sums[:3]]
        grav_out[...] = jnp.where(sub == 0, accel[0], jnp.where(sub == 1, accel[1], accel[2]))
        offset = sums[3].astype(jnp.int32) - me * held + 1
        info_out[...] = jnp.where(lane == 0, offset, sums[4].astype(jnp.int32))

        def advance(p, ref, own_faces, far, from_low, write):
            level = jnp.full((ROWS, LANES), levels[p].astype(jnp.float32))
            half_ratio = 0.0125 * jnp.exp2(level)
            g = [
                DT_STEP * jnp.broadcast_to(
                    jnp.sum(jnp.where(lane == p, accel[a], 0.0), axis=1, keepdims=True),
                    (ROWS, LANES),
                )
                for a in range(3)
            ]

            def ghost(f, axis):
                nb = neighbors[p, f]
                base = held * (1 - f % 2)
                near = jnp.where(nb >= 0, base + jnp.clip(nb - me * held, 0, held - 1),
                                 held * (f % 2) + p)
                out = [own_faces[near, axis, i] for i in range(FIELDS)]
                if from_low == (f % 2 == 0):
                    if from_low:
                        slot, away = nb - me * held + window, (nb >= 0) & (nb < me * held)
                    else:
                        slot, away = nb - (me + 1) * held, nb >= (me + 1) * held
                    slot = jnp.clip(slot, 0, window - 1)
                    out = [jnp.where(away, far[slot, axis, i], out[i]) for i in range(FIELDS)]
                return out

            def own(high, axis):
                base = held * int(high) + p
                return [own_faces[base, axis, i] for i in range(FIELDS)]

            z_low = interface(with_flux(ghost(4, 2), 2), with_flux(own(False, 2), 2))
            z_high = interface(with_flux(own(True, 2), 2), with_flux(ghost(5, 2), 2))
            y_low = interface(with_flux(ghost(2, 1), 1), with_flux(own(False, 1), 1))
            y_high = interface(with_flux(own(True, 1), 1), with_flux(ghost(3, 1), 1))
            for f in range(FIELDS):
                turned = pltpu.roll(z_high[f], EDGE - 1, 1)
                edge_z[0, f] = jnp.where((lane & 1) == 0, z_low[f], turned)
                edge_z[1, f] = jnp.where((lane & 1) == 1, z_low[f], turned)
                for q in range(4):
                    low = y_low[f] if q == 0 else pltpu.roll(y_low[f], LANES - 32 * q, 1)
                    high = y_high[f] if q == 3 else pltpu.roll(y_high[f], 96 - 32 * q, 1)
                    edge_y[0, f, pl.ds(q * ROWS, ROWS), :] = low
                    edge_y[1, f, pl.ds(q * ROWS, ROWS), :] = high
            before = with_flux(ghost(0, 0), 0)
            pending = [zero] * FIELDS

            at_z0 = lane_z == 0
            at_z31 = lane_z == EDGE - 1
            at_y0 = (sub == 0) & (lane < 32)
            at_y31 = (sub == ROWS - 1) & (lane >= 96)
            carry_high = lane >= 96

            def back_z(v):
                return pltpu.roll(v, 1, 1)

            def ahead_z(v):
                return pltpu.roll(v, LANES - 1, 1)

            def ahead_y(v):
                t = pltpu.roll(v, LANES - 32, 1)
                return jnp.where(carry_high, pltpu.roll(t, ROWS - 1, 0), t)

            def shifted(u, f, s, k, move):
                mu = [move(v) for v in u]
                mf = [mu[k + 1]] + [move(v) for v in f[1:]]
                return mu, mf, move(s)

            def one(x, odd, before, pending):
                u = [plane(ref, p, f, x) for f in range(FIELDS)]
                prim = primitives(u)
                fx, sx = flux(u, prim, 0)
                gx = interface(before, (u, fx, sx))
                write(p, jnp.maximum(x - 1, 0),
                      [pending[f] - half_ratio * gx[f] for f in range(FIELDS)])
                fy, sy = flux(u, prim, 1)
                rows = [plane_back(ref, p, f, x) for f in range(FIELDS)]
                below = [pltpu.roll(jnp.where(carry_high, rows[f], u[f]), 32, 1) for f in range(FIELDS)]
                gy = interface(with_flux(below, 1), (u, fy, sy))
                fz, sz = flux(u, prim, 2)
                gz = interface(shifted(u, fz, sz, 2, back_z), (u, fz, sz))
                fresh = []
                for f in range(FIELDS):
                    ey0 = edge_y[0, f, pl.ds(x, 1), :]
                    ey1 = edge_y[1, f, pl.ds(x, 1), :]
                    ez = pltpu.roll(edge_z[odd, f], LANES - x, 1)
                    div = jnp.where(at_y31, ey1, ahead_y(gy[f])) - jnp.where(at_y0, ey0, gy[f])
                    div += jnp.where(at_z31, ez, ahead_z(gz[f])) - jnp.where(at_z0, ez, gz[f])
                    fresh.append(u[f] - half_ratio * (div - gx[f]))
                for a in range(3):
                    fresh[a + 1] += u[0] * g[a]
                fresh[4] += u[1] * g[0] + u[2] * g[1] + u[3] * g[2]
                return (u, fx, sx), fresh

            def block(xb, carry):
                bu, bf, bs, pend = carry
                before, pend = (list(bu), list(bf), bs), list(pend)
                for i in range(UNROLL):
                    before, pend = one(xb * UNROLL + i, i % 2, before, pend)
                return tuple(before[0]), tuple(before[1]), before[2], tuple(pend)

            carry = (tuple(before[0]), tuple(before[1]), before[2], tuple(pending))
            bu, bf, bs, pend = lax.fori_loop(0, PLANES // UNROLL, block, carry)
            gx = interface((bu, bf, bs), with_flux(ghost(1, 0), 0))
            write(p, PLANES - 1, [pend[f] - half_ratio * gx[f] for f in range(FIELDS)])

        def rows_of(x):
            return pl.ds(pl.multiple_of(x * ROWS, ROWS), ROWS)

        def write_one(p, x, values):
            for f in range(FIELDS):
                s1[p, f, pl.ds(pl.multiple_of(x * ROWS + PAD, ROWS), ROWS), :] = values[f]

        def write_two(p, x, values):
            for f in range(FIELDS):
                fin[p, f, rows_of(x), :] = 0.5 * (plane(u0, p, f, x) + values[f])

        wait_from_low(pair1)
        wait_from_high(pair1)
        pair2 = face_copies(own2, low2, high2, f_send.at[1], f_recv.at[1])

        def stage_one(far, from_low):
            def step(p, _):
                advance(p, u0, own1, far, from_low, write_one)
                pack_faces(p, s1, own2)
                return 0

            return step

        lax.fori_loop(0, window, stage_one(low1, True), 0)
        start_down(pair2)
        lax.fori_loop(window, held, stage_one(high1, False), 0)
        start_up(pair2)

        def patch_copies():
            down = pltpu.make_async_remote_copy(
                src_ref=fin.at[0], dst_ref=ext.at[held + 1],
                send_sem=g_send.at[0], recv_sem=g_recv.at[0],
                device_id=(run, me - 1), device_id_type=pl.DeviceIdType.MESH,
            )
            up = pltpu.make_async_remote_copy(
                src_ref=fin.at[held - 1], dst_ref=ext.at[0],
                send_sem=g_send.at[1], recv_sem=g_recv.at[1],
                device_id=(run, me + 1), device_id_type=pl.DeviceIdType.MESH,
            )
            return down, up

        pair3 = patch_copies()

        def keep(p):
            return pltpu.make_async_copy(fin.at[p], ext.at[p + 1], out_sem.at[p])

        def stage_two(p, far, from_low):
            advance(p, s1, own2, far, from_low, write_two)
            keep(p).start()

        wait_from_high(pair2)
        stage_two(held - 1, high2, False)
        start_up(pair3)
        wait_from_low(pair2)
        stage_two(0, low2, True)
        start_down(pair3)

        def inner_high(i, _):
            stage_two(i, high2, False)
            return 0

        def inner_low(i, _):
            stage_two(i, low2, True)
            return 0

        lax.fori_loop(window, held - 1, inner_high, 0)
        lax.fori_loop(1, window, inner_low, 0)
        for pair in (pair1, pair2, pair3):
            wait_sent(pair)
        wait_from_low(pair3)
        wait_from_high(pair3)
        for p in range(held):
            keep(p).wait()

    return kernel


def place_kernel(info, source, grav, out, grav_out):
    last = source.shape[0] - 1
    offset, count = info[0, 0], info[0, 1]
    sub, _ = iotas()
    used = sub < count
    at = [jnp.minimum(slot + offset, last) for slot in range(CAP)]

    def step(rb, _):
        for i in range(16):
            row = rb * 16 + i
            tile = jnp.zeros((ROWS, LANES), jnp.float32)
            for slot in range(CAP):
                line = jnp.broadcast_to(source[at[slot], 0, pl.ds(row, 1), :], (ROWS, LANES))
                tile = line if slot == 0 else jnp.where(sub == slot, line, tile)
            out[0, row] = jnp.where(used, tile, 0.0)[:CAP]
        return 0

    lax.fori_loop(0, TILES // 16, step, 0)
    grav_out[...] = grav[: grav_out.shape[0], : grav_out.shape[1]]


def local(state, levels, neighbors, new_counts):
    held = state.shape[0]
    devices = lax.axis_size("patch")
    tiles = state.transpose(1, 0, 2).reshape(FIELDS, held, TILES, LANES).transpose(0, 2, 1, 3)
    tiles = tiles.reshape(FIELDS, TILES * held, LANES)
    f32 = jnp.float32
    smem = pl.BlockSpec(memory_space=pltpu.SMEM)
    vmem = pl.BlockSpec(memory_space=pltpu.VMEM)
    anyspace = pl.BlockSpec(memory_space=pl.ANY)
    padded = (held, FIELDS, TILES + PAD, LANES)
    dense = (held, FIELDS, TILES, LANES)
    faces = (2 * held, 3, FIELDS, ROWS, LANES)
    far = (held // 2,) + faces[1:]
    dma = pltpu.SemaphoreType.DMA
    ext, grav, info = pl.pallas_call(
        make_kernel(devices, held),
        out_shape=(
            jax.ShapeDtypeStruct((held + 2, FIELDS, TILES, LANES), f32),
            jax.ShapeDtypeStruct((ROWS, LANES), f32),
            jax.ShapeDtypeStruct((ROWS, LANES), jnp.int32),
        ),
        in_specs=[anyspace, smem, smem, smem],
        out_specs=(anyspace, vmem, vmem),
        scratch_shapes=[
            pltpu.VMEM((FIELDS, TILES * held, LANES), f32),
            pltpu.VMEM(padded, f32),
            pltpu.VMEM(padded, f32),
            pltpu.VMEM(dense, f32),
            pltpu.VMEM(faces, f32), pltpu.VMEM(far, f32), pltpu.VMEM(far, f32),
            pltpu.VMEM(faces, f32), pltpu.VMEM(far, f32), pltpu.VMEM(far, f32),
            pltpu.VMEM((ROWS, LANES), f32),
            pltpu.VMEM((devices, ROWS, LANES), f32),
            pltpu.VMEM((2, FIELDS, ROWS, LANES), f32),
            pltpu.VMEM((2, FIELDS, EDGE, LANES), f32),
            dma((FIELDS,)), dma((held,)),
            dma((devices,)), dma((devices,)),
            dma((2, 2)), dma((2, 2)),
            dma((2,)), dma((2,)),
        ],
        compiler_params=pltpu.CompilerParams(
            collective_id=0, has_side_effects=True, vmem_limit_bytes=60 * 2**20
        ),
        name="advance",
    )(tiles, levels, neighbors.T, new_counts)
    out, gravity = pl.pallas_call(
        place_kernel,
        out_shape=(
            jax.ShapeDtypeStruct((FIELDS, TILES, CAP, LANES), f32),
            jax.ShapeDtypeStruct((3, held), f32),
        ),
        grid_spec=pltpu.PrefetchScalarGridSpec(
            num_scalar_prefetch=1,
            grid=(FIELDS,),
            in_specs=[
                pl.BlockSpec(
                    (held + 2, 1, TILES, LANES),
                    lambda f, info: (0, f, 0, 0),
                ),
                pl.BlockSpec((ROWS, LANES), lambda f, info: (0, 0)),
            ],
            out_specs=(
                pl.BlockSpec((1, TILES, CAP, LANES), lambda f, info: (f, 0, 0, 0)),
                pl.BlockSpec((3, held), lambda f, info: (0, 0)),
            ),
        ),
        compiler_params=pltpu.CompilerParams(vmem_limit_bytes=60 * 2**20),
        name="place",
    )(info, ext, grav)
    advanced = out.transpose(0, 2, 1, 3).reshape(FIELDS, CAP, TILES * LANES).transpose(1, 0, 2)
    return advanced, gravity


def solution(mesh):
    return jax.shard_map(
        local,
        mesh=mesh,
        in_specs=(
            P(("runs", "patch"), None, None),
            P(("runs", "patch")),
            P(None, ("runs", "patch")),
            P(("runs", "patch")),
        ),
        out_specs=(P(("runs", "patch"), None, None), P(None, ("runs", "patch"))),
        check_vma=False,
    )
```

```python
import jax
import jax.numpy as jnp
from jax import lax
from jax.experimental import pallas as pl
from jax.experimental.pallas import tpu as pltpu
from jax.sharding import PartitionSpec as P

FIELDS = 5
EDGE = 32
CAP = 6
LANES = 128
ROWS = 8
PLANES = 32
TILES = 256
PAD = 8

GAMMA = 1.4
DT_STEP = 0.01
GRAV_C = 2.0
SOFTEN = 0.25
UNROLL = 4


def primitives(u):
    density, m1, m2, m3, energy = u
    inverse = pl.reciprocal(density, approx=True)
    inverse = inverse * (2.0 - density * inverse)
    velocity = [m1 * inverse, m2 * inverse, m3 * inverse]
    twice_kinetic = m1 * velocity[0] + m2 * velocity[1] + m3 * velocity[2]
    pressure = (GAMMA - 1.0) * energy - (0.5 * (GAMMA - 1.0)) * twice_kinetic
    square = GAMMA * pressure * inverse
    sound = square * lax.rsqrt(jnp.maximum(square, 1e-30))
    return velocity, pressure, sound, energy + pressure


def flux(u, prim, k):
    velocity, pressure, sound, enthalpy = prim
    speed = velocity[k]
    out = [u[k + 1]]
    for c in range(3):
        term = u[c + 1] * speed
        out.append(term + pressure if c == k else term)
    out.append(enthalpy * speed)
    return out, jnp.abs(speed) + sound


def interface(lower, upper):
    u_l, f_l, s_l = lower
    u_r, f_r, s_r = upper
    wave = jnp.maximum(s_l, s_r)
    return [(f_l[i] + f_r[i]) - wave * (u_r[i] - u_l[i]) for i in range(FIELDS)]


def with_flux(u, k):
    f, s = flux(u, primitives(u), k)
    return u, f, s


def iotas():
    sub = lax.broadcasted_iota(jnp.int32, (ROWS, LANES), 0)
    lane = lax.broadcasted_iota(jnp.int32, (ROWS, LANES), 1)
    return sub, lane


def curve_coords(positions, bits):
    coords = [jnp.zeros_like(positions) for _ in range(3)]
    for b in range(bits):
        coords[b % 3] = coords[b % 3] + ((positions >> b) & 1) * 2 ** (b // 3)
    return [c.astype(jnp.float32) for c in coords]


def make_kernel(devices, held):
    npatch = devices * held
    bits = npatch.bit_length() - 1
    strength = GRAV_C / float(npatch) ** (1.0 / 3.0)
    window = held // 2

    def kernel(
        state, levels, neighbors, counts,
        ext, grav_out, info_out,
        tin, u0, s1, fin, own1, low1, high1, own2, low2, high2, msg, gath, edge_z, edge_y,
        in_sem, out_sem, mass_send, mass_recv, f_send, f_recv, g_send, g_recv,
    ):
        me = lax.axis_index("patch")
        run = lax.axis_index("runs")
        sub, lane = iotas()
        lane_z = lane & (EDGE - 1)
        has_low = me > 0
        has_high = me < devices - 1

        loads = [
            pltpu.make_async_copy(state.at[f], tin.at[f], in_sem.at[f]) for f in range(FIELDS)
        ]
        for c in loads:
            c.start()

        barrier = pltpu.get_barrier_semaphore()

        def greet(i, _):
            pl.semaphore_signal(
                barrier, inc=1, device_id=(run, lax.rem(me + i, devices)),
                device_id_type=pl.DeviceIdType.MESH,
            )
            return 0

        lax.fori_loop(1, devices, greet, 0)
        def plane(ref, p, f, x):
            return ref[p, f, pl.ds(pl.multiple_of(x * ROWS + PAD, ROWS), ROWS), :]

        def plane_back(ref, p, f, x):
            return ref[p, f, pl.ds(pl.multiple_of(x * ROWS, ROWS) + (PAD - 1), ROWS), :]

        def pack_faces(p, ref, faces):
            for f in range(FIELDS):
                faces[p, 0, f] = ref[p, f, pl.ds(PAD, ROWS), :]
                faces[held + p, 0, f] = ref[p, f, pl.ds(PAD + (PLANES - 1) * ROWS, ROWS), :]
                low_y = ref[p, f, pl.ds(PAD, ROWS, stride=ROWS), :]
                high_y = pltpu.roll(ref[p, f, pl.ds(PAD + ROWS - 1, ROWS, stride=ROWS), :], 32, 1)
                for g in range(1, 4):
                    at = PAD + g * ROWS * ROWS
                    inside = (lane >> 5) == g
                    more = ref[p, f, pl.ds(at, ROWS, stride=ROWS), :]
                    low_y = jnp.where(inside, pltpu.roll(more, 32 * g, 1), low_y)
                    more = ref[p, f, pl.ds(at + ROWS - 1, ROWS, stride=ROWS), :]
                    high_y = jnp.where(inside, pltpu.roll(more, 32 * (g + 1) % LANES, 1), high_y)
                faces[p, 1, f] = low_y
                faces[held + p, 1, f] = high_y
                low_z = ref[p, f, pl.ds(PAD, ROWS), :]
                high_z = pltpu.roll(low_z, LANES - 31, 1)
                for x in range(1, PLANES):
                    here = lane_z == x
                    now = ref[p, f, pl.ds(PAD + x * ROWS, ROWS), :]
                    low_z = jnp.where(here, pltpu.roll(now, x, 1), low_z)
                    turned = now if x == 31 else pltpu.roll(now, LANES + x - 31, 1)
                    high_z = jnp.where(here, turned, high_z)
                faces[p, 2, f] = low_z
                faces[held + p, 2, f] = high_z

        def unpack(f):
            def step(xb, totals):
                totals = list(totals)
                for i in range(8):
                    x = xb * 8 + i
                    at = pl.ds(pl.multiple_of(x * ROWS + PAD, ROWS), ROWS)
                    for p in range(held):
                        v = tin[f, pl.ds(x * (held * ROWS) + p, ROWS, stride=held), :]
                        u0[p, f, at, :] = v
                        if f == 0:
                            totals[p] = totals[p] + v
                return tuple(totals)

            loads[f].wait()
            return lax.fori_loop(0, PLANES // 8, step, (zero,) * held if f == 0 else ())

        zero = jnp.zeros((ROWS, LANES), jnp.float32)
        totals = unpack(0)
        message = jnp.where(sub == held, counts[0].astype(jnp.float32), 0.0)
        for p in range(held):
            total = jnp.sum(jnp.sum(totals[p], axis=0, keepdims=True), axis=1, keepdims=True)
            level = jnp.full((ROWS, LANES), levels[p].astype(jnp.float32))
            mass = jnp.broadcast_to(total, (ROWS, LANES)) * (1.0 / (LANES * TILES))
            message = jnp.where(sub == p, mass * jnp.exp2(-3.0 * level), message)
        msg[...] = message
        gath[me] = message
        pl.semaphore_wait(barrier, devices - 1)

        def mass_copy(target, slot, s_sem, r_sem):
            return pltpu.make_async_remote_copy(
                src_ref=msg, dst_ref=gath.at[slot], send_sem=s_sem, recv_sem=r_sem,
                device_id=(run, target), device_id_type=pl.DeviceIdType.MESH,
            )

        def face_copies(own, low, high, send, recv):
            down = pltpu.make_async_remote_copy(
                src_ref=own.at[pl.ds(0, window)], dst_ref=high,
                send_sem=send.at[0], recv_sem=recv.at[0],
                device_id=(run, me - 1), device_id_type=pl.DeviceIdType.MESH,
            )
            up = pltpu.make_async_remote_copy(
                src_ref=own.at[pl.ds(2 * held - window, window)], dst_ref=low,
                send_sem=send.at[1], recv_sem=recv.at[1],
                device_id=(run, me + 1), device_id_type=pl.DeviceIdType.MESH,
            )
            return down, up

        def start_down(pair):
            pl.when(has_low)(lambda: pair[0].start())

        def start_up(pair):
            pl.when(has_high)(lambda: pair[1].start())

        def wait_sent(pair):
            pl.when(has_low)(lambda: pair[0].wait_send())
            pl.when(has_high)(lambda: pair[1].wait_send())

        def wait_from_high(pair):
            pl.when(has_high)(lambda: pair[0].wait_recv())

        def wait_from_low(pair):
            pl.when(has_low)(lambda: pair[1].wait_recv())

        def send_mass(i, _):
            target = lax.rem(me + i, devices)
            mass_copy(target, me, mass_send.at[i], mass_recv.at[me]).start()
            return 0

        lax.fori_loop(1, devices, send_mass, 0)
        for f in range(1, FIELDS):
            unpack(f)

        def pack_first(p, _):
            pack_faces(p, u0, own1)
            return 0

        lax.fori_loop(0, held, pack_first, 0)
        pair1 = face_copies(own1, low1, high1, f_send.at[0], f_recv.at[0])
        start_down(pair1)
        start_up(pair1)

        def wait_mass(i, _):
            source = lax.rem(me + i, devices)
            c = mass_copy(source, source, mass_send.at[i], mass_recv.at[source])
            c.wait_send()
            c.wait_recv()
            return 0

        lax.fori_loop(1, devices, wait_mass, 0)

        target = curve_coords(me * held + (lane & (held - 1)), bits)

        def pull(j, sums):
            got_mass = gath[j]
            source = curve_coords(j * held + (sub & (held - 1)), bits)
            off = [source[a] - target[a] for a in range(3)]
            d = off[0] * off[0] + off[1] * off[1] + off[2] * off[2] + SOFTEN
            inv = lax.rsqrt(d)
            w = jnp.where(sub < held, got_mass, 0.0) * (inv * inv * inv)
            is_count = sub == held
            start = sums[3] + jnp.where(is_count & (j < me), got_mass, 0.0)
            count = sums[4] + jnp.where(is_count & (j == me), got_mass, 0.0)
            return tuple(sums[a] + w * off[a] for a in range(3)) + (start, count)

        group = 4 if devices % 4 == 0 else 1

        def pull_group(jb, sums):
            for i in range(group):
                sums = pull(jb * group + i, sums)
            return sums

        sums = lax.fori_loop(0, devices // group, pull_group, (zero,) * 5)
        sums = [jnp.broadcast_to(jnp.sum(s, axis=0, keepdims=True), (ROWS, LANES)) for s in sums]
        accel = [strength * s for s in sums[:3]]
        grav_out[...] = jnp.where(sub == 0, accel[0], jnp.where(sub == 1, accel[1], accel[2]))
        offset = jnp.clip(sums[3].astype(jnp.int32) - me * held + 1, 0, CAP - held)
        info_out[...] = jnp.where(lane == 0, offset, sums[4].astype(jnp.int32))

        def advance(p, ref, own_faces, far, from_low, write):
            level = jnp.full((ROWS, LANES), levels[p].astype(jnp.float32))
            half_ratio = 0.0125 * jnp.exp2(level)
            g = [
                DT_STEP * jnp.broadcast_to(
                    jnp.sum(jnp.where(lane == p, accel[a], 0.0), axis=1, keepdims=True),
                    (ROWS, LANES),
                )
                for a in range(3)
            ]

            def ghost(f, axis):
                nb = neighbors[p, f]
                base = held * (1 - f % 2)
                near = jnp.where(nb >= 0, base + jnp.clip(nb - me * held, 0, held - 1),
                                 held * (f % 2) + p)
                out = [own_faces[near, axis, i] for i in range(FIELDS)]
                if from_low == (f % 2 == 0):
                    if from_low:
                        slot, away = nb - me * held + window, (nb >= 0) & (nb < me * held)
                    else:
                        slot, away = nb - (me + 1) * held, nb >= (me + 1) * held
                    slot = jnp.clip(slot, 0, window - 1)
                    out = [jnp.where(away, far[slot, axis, i], out[i]) for i in range(FIELDS)]
                return out

            def own(high, axis):
                base = held * int(high) + p
                return [own_faces[base, axis, i] for i in range(FIELDS)]

            z_low = interface(with_flux(ghost(4, 2), 2), with_flux(own(False, 2), 2))
            z_high = interface(with_flux(own(True, 2), 2), with_flux(ghost(5, 2), 2))
            y_low = interface(with_flux(ghost(2, 1), 1), with_flux(own(False, 1), 1))
            y_high = interface(with_flux(own(True, 1), 1), with_flux(ghost(3, 1), 1))
            for f in range(FIELDS):
                turned = pltpu.roll(z_high[f], EDGE - 1, 1)
                edge_z[0, f] = jnp.where((lane & 1) == 0, z_low[f], turned)
                edge_z[1, f] = jnp.where((lane & 1) == 1, z_low[f], turned)
                for q in range(4):
                    low = y_low[f] if q == 0 else pltpu.roll(y_low[f], LANES - 32 * q, 1)
                    high = y_high[f] if q == 3 else pltpu.roll(y_high[f], 96 - 32 * q, 1)
                    edge_y[0, f, pl.ds(q * ROWS, ROWS), :] = low
                    edge_y[1, f, pl.ds(q * ROWS, ROWS), :] = high
            before = with_flux(ghost(0, 0), 0)
            pending = [zero] * FIELDS

            at_z0 = lane_z == 0
            at_z31 = lane_z == EDGE - 1
            at_y0 = (sub == 0) & (lane < 32)
            at_y31 = (sub == ROWS - 1) & (lane >= 96)
            carry_high = lane >= 96

            def back_z(v):
                return pltpu.roll(v, 1, 1)

            def ahead_z(v):
                return pltpu.roll(v, LANES - 1, 1)

            def ahead_y(v):
                t = pltpu.roll(v, LANES - 32, 1)
                return jnp.where(carry_high, pltpu.roll(t, ROWS - 1, 0), t)

            def shifted(u, f, s, k, move):
                mu = [move(v) for v in u]
                mf = [mu[k + 1]] + [move(v) for v in f[1:]]
                return mu, mf, move(s)

            def one(x, odd, before, pending):
                u = [plane(ref, p, f, x) for f in range(FIELDS)]
                prim = primitives(u)
                fx, sx = flux(u, prim, 0)
                gx = interface(before, (u, fx, sx))
                write(p, jnp.maximum(x - 1, 0),
                      [pending[f] - half_ratio * gx[f] for f in range(FIELDS)])
                fy, sy = flux(u, prim, 1)
                rows = [plane_back(ref, p, f, x) for f in range(FIELDS)]
                below = [pltpu.roll(jnp.where(carry_high, rows[f], u[f]), 32, 1) for f in range(FIELDS)]
                gy = interface(with_flux(below, 1), (u, fy, sy))
                fz, sz = flux(u, prim, 2)
                gz = interface(shifted(u, fz, sz, 2, back_z), (u, fz, sz))
                fresh = []
                for f in range(FIELDS):
                    ey0 = edge_y[0, f, pl.ds(x, 1), :]
                    ey1 = edge_y[1, f, pl.ds(x, 1), :]
                    ez = pltpu.roll(edge_z[odd, f], LANES - x, 1)
                    div = jnp.where(at_y31, ey1, ahead_y(gy[f])) - jnp.where(at_y0, ey0, gy[f])
                    div += jnp.where(at_z31, ez, ahead_z(gz[f])) - jnp.where(at_z0, ez, gz[f])
                    fresh.append(u[f] - half_ratio * (div - gx[f]))
                for a in range(3):
                    fresh[a + 1] += u[0] * g[a]
                fresh[4] += u[1] * g[0] + u[2] * g[1] + u[3] * g[2]
                return (u, fx, sx), fresh

            def block(xb, carry):
                bu, bf, bs, pend = carry
                before, pend = (list(bu), list(bf), bs), list(pend)
                for i in range(UNROLL):
                    before, pend = one(xb * UNROLL + i, i % 2, before, pend)
                return tuple(before[0]), tuple(before[1]), before[2], tuple(pend)

            carry = (tuple(before[0]), tuple(before[1]), before[2], tuple(pending))
            bu, bf, bs, pend = lax.fori_loop(0, PLANES // UNROLL, block, carry)
            gx = interface((bu, bf, bs), with_flux(ghost(1, 0), 0))
            write(p, PLANES - 1, [pend[f] - half_ratio * gx[f] for f in range(FIELDS)])

        def rows_of(x):
            return pl.ds(pl.multiple_of(x * ROWS, ROWS), ROWS)

        def write_one(p, x, values):
            for f in range(FIELDS):
                s1[p, f, pl.ds(pl.multiple_of(x * ROWS + PAD, ROWS), ROWS), :] = values[f]

        def write_two(p, x, values):
            for f in range(FIELDS):
                fin[p, f, rows_of(x), :] = 0.5 * (plane(u0, p, f, x) + values[f])

        wait_from_low(pair1)
        wait_from_high(pair1)
        pair2 = face_copies(own2, low2, high2, f_send.at[1], f_recv.at[1])

        def stage_one(far, from_low):
            def step(p, _):
                advance(p, u0, own1, far, from_low, write_one)
                pack_faces(p, s1, own2)
                return 0

            return step

        lax.fori_loop(0, window, stage_one(low1, True), 0)
        start_down(pair2)
        lax.fori_loop(window, held, stage_one(high1, False), 0)
        start_up(pair2)

        def patch_copies():
            down = pltpu.make_async_remote_copy(
                src_ref=fin.at[0], dst_ref=ext.at[held + 1],
                send_sem=g_send.at[0], recv_sem=g_recv.at[0],
                device_id=(run, me - 1), device_id_type=pl.DeviceIdType.MESH,
            )
            up = pltpu.make_async_remote_copy(
                src_ref=fin.at[held - 1], dst_ref=ext.at[0],
                send_sem=g_send.at[1], recv_sem=g_recv.at[1],
                device_id=(run, me + 1), device_id_type=pl.DeviceIdType.MESH,
            )
            return down, up

        pair3 = patch_copies()

        def keep(p):
            return pltpu.make_async_copy(fin.at[p], ext.at[p + 1], out_sem.at[p])

        def stage_two(p, far, from_low):
            advance(p, s1, own2, far, from_low, write_two)
            keep(p).start()

        wait_from_high(pair2)
        stage_two(held - 1, high2, False)
        start_up(pair3)
        wait_from_low(pair2)
        stage_two(0, low2, True)
        start_down(pair3)

        def inner_high(i, _):
            stage_two(i, high2, False)
            return 0

        def inner_low(i, _):
            stage_two(i, low2, True)
            return 0

        lax.fori_loop(window, held - 1, inner_high, 0)
        lax.fori_loop(1, window, inner_low, 0)
        for pair in (pair1, pair2, pair3):
            wait_sent(pair)
        wait_from_low(pair3)
        wait_from_high(pair3)
        for p in range(held):
            keep(p).wait()

    return kernel


def place_kernel(info, source, grav, out, grav_out):
    last = source.shape[0] - 1
    offset, count = info[0, 0], info[0, 1]
    sub, _ = iotas()
    used = sub < count
    at = [jnp.minimum(slot + offset, last) for slot in range(CAP)]

    def step(rb, _):
        for i in range(16):
            row = rb * 16 + i
            tile = jnp.zeros((ROWS, LANES), jnp.float32)
            for slot in range(CAP):
                line = jnp.broadcast_to(source[at[slot], 0, pl.ds(row, 1), :], (ROWS, LANES))
                tile = line if slot == 0 else jnp.where(sub == slot, line, tile)
            out[0, row] = jnp.where(used, tile, 0.0)[:CAP]
        return 0

    lax.fori_loop(0, out.shape[1] // 16, step, 0)
    grav_out[...] = grav[: grav_out.shape[0], : grav_out.shape[1]]


def local(state, levels, neighbors, new_counts):
    held = state.shape[0]
    devices = lax.axis_size("patch")
    tiles = state.transpose(1, 0, 2).reshape(FIELDS, held, TILES, LANES).transpose(0, 2, 1, 3)
    tiles = tiles.reshape(FIELDS, TILES * held, LANES)
    f32 = jnp.float32
    smem = pl.BlockSpec(memory_space=pltpu.SMEM)
    vmem = pl.BlockSpec(memory_space=pltpu.VMEM)
    anyspace = pl.BlockSpec(memory_space=pl.ANY)
    padded = (held, FIELDS, TILES + PAD, LANES)
    dense = (held, FIELDS, TILES, LANES)
    faces = (2 * held, 3, FIELDS, ROWS, LANES)
    far = (held // 2,) + faces[1:]
    dma = pltpu.SemaphoreType.DMA
    ext, grav, info = pl.pallas_call(
        make_kernel(devices, held),
        out_shape=(
            jax.ShapeDtypeStruct((held + 2, FIELDS, TILES, LANES), f32),
            jax.ShapeDtypeStruct((ROWS, LANES), f32),
            jax.ShapeDtypeStruct((ROWS, LANES), jnp.int32),
        ),
        in_specs=[anyspace, smem, smem, smem],
        out_specs=(anyspace, vmem, vmem),
        scratch_shapes=[
            pltpu.VMEM((FIELDS, TILES * held, LANES), f32),
            pltpu.VMEM(padded, f32),
            pltpu.VMEM(padded, f32),
            pltpu.VMEM(dense, f32),
            pltpu.VMEM(faces, f32), pltpu.VMEM(far, f32), pltpu.VMEM(far, f32),
            pltpu.VMEM(faces, f32), pltpu.VMEM(far, f32), pltpu.VMEM(far, f32),
            pltpu.VMEM((ROWS, LANES), f32),
            pltpu.VMEM((devices, ROWS, LANES), f32),
            pltpu.VMEM((2, FIELDS, ROWS, LANES), f32),
            pltpu.VMEM((2, FIELDS, EDGE, LANES), f32),
            dma((FIELDS,)), dma((held,)),
            dma((devices,)), dma((devices,)),
            dma((2, 2)), dma((2, 2)),
            dma((2,)), dma((2,)),
        ],
        compiler_params=pltpu.CompilerParams(
            collective_id=0, has_side_effects=True, vmem_limit_bytes=60 * 2**20
        ),
        name="advance",
    )(tiles, levels, neighbors.T, new_counts)
    out, gravity = pl.pallas_call(
        place_kernel,
        out_shape=(
            jax.ShapeDtypeStruct((FIELDS, TILES, CAP, LANES), f32),
            jax.ShapeDtypeStruct((3, held), f32),
        ),
        grid_spec=pltpu.PrefetchScalarGridSpec(
            num_scalar_prefetch=1,
            grid=(FIELDS, 2),
            in_specs=[
                pl.BlockSpec(
                    (held + 2, 1, TILES // 2, LANES),
                    lambda f, h, info: (0, f, h, 0),
                ),
                pl.BlockSpec((ROWS, LANES), lambda f, h, info: (0, 0)),
            ],
            out_specs=(
                pl.BlockSpec((1, TILES // 2, CAP, LANES), lambda f, h, info: (f, h, 0, 0)),
                pl.BlockSpec((3, held), lambda f, h, info: (0, 0)),
            ),
        ),
        compiler_params=pltpu.CompilerParams(vmem_limit_bytes=60 * 2**20),
        name="place",
    )(info, ext, grav)
    advanced = out.transpose(0, 2, 1, 3).reshape(FIELDS, CAP, TILES * LANES).transpose(1, 0, 2)
    return advanced, gravity


def solution(mesh):
    return jax.shard_map(
        local,
        mesh=mesh,
        in_specs=(
            P(("runs", "patch"), None, None),
            P(("runs", "patch")),
            P(None, ("runs", "patch")),
            P(("runs", "patch")),
        ),
        out_specs=(P(("runs", "patch"), None, None), P(None, ("runs", "patch"))),
        check_vma=False,
    )
```
